32 devices in a mesh: blk: 8 (over z, y), team: 4 (over x, core).
Axes of the slice: x: 2, y: 2, z: 4, core: 2. Of those that a mesh axis runs over, the one named last changes fastest.
Arguments:
- loadings: bfloat16 [64, 98304], P(None, ('blk', 'team')), may hold values from -6 to 6
- scales: bfloat16 [64, 768], P(None, ('blk', 'team')), may hold values from 0.25 to 4
- cov: bfloat16 [2048, 2, 4, 12288], P('blk', None, 'team'), may hold values from -0.01953125 to 0.01953125
Outputs:
- product: float32 [64, 2048], P(None, 'blk')
The draws below stay inside these ranges and needn't reach their ends.
All inputs are finite; a program needn't handle non-finite values.
Results may differ from the reference program's by a relative error of at most 0.0028.
Values may be sent and summed in bfloat16 or wider, within the bound.
A program may use at most 128 MiB of HBM per device.

```python
import math
import jax
import jax.numpy as jnp
from jax import lax

M = 98304
K = 64
GROUP = 128
ROWS = 2048
STOPS = 2
BLOCK = 12288
N_TEAM = 4


def steps_of(key, dims, pieces, smallest, largest):
    loudness, own = 1.0, jax.random.fold_in(key, 6)
    for dim, blocks in pieces:
        heights = jnp.exp(jax.random.uniform(jax.random.fold_in(own, dim), (blocks,), jnp.float32, smallest / len(pieces), largest / len(pieces)))
        loudness = loudness * jnp.repeat(heights, dims[dim] // blocks).reshape([-1 if axis == dim else 1 for axis in range(len(dims))])
    return loudness


def normal_values(rng, dims, scale, bound, shards=(), held_as=jnp.bfloat16):
    factor_of = steps_of(rng, dims, shards, -0.22, 0.18) if shards else 1.0
    entries = jax.random.normal(rng, dims, jnp.float32) * scale * factor_of
    return jnp.minimum(jnp.maximum(entries, -bound), bound).astype(held_as)


def setup_inputs(seed: int = 0) -> dict:
    key_of = jax.random.split(jax.random.key(seed), 4)
    return {
        "loadings": normal_values(key_of[0], (K, M), 1.0, 6.0, ((1, 32),)),
        "scales": jnp.clip(jnp.exp(math.log(4.0) - 2.7725887 * jax.random.uniform(key_of[1], (K, M // GROUP), jnp.float32) ** steps_of(key_of[1], (K, M // GROUP), ((1, 32),), -0.2, 0.2)), 0.25, 4.0).astype(jnp.bfloat16),
        "cov": normal_values(key_of[2], (ROWS, STOPS, N_TEAM, BLOCK), M ** -0.5, 0.01953125, ((0, 8), (2, 4))),
    }


def reference(loadings, scales, cov):
    n_loads = loadings.shape[0]
    n_cols = loadings.shape[1]
    scaled = (loadings.astype(jnp.float32).reshape(n_loads, n_cols // GROUP, GROUP) * scales.astype(jnp.float32)[:, :, None]).reshape(n_loads, n_cols).astype(jnp.bfloat16)
    cov_rows = cov.reshape(ROWS, M)
    col_width = math.gcd(M, 8192)
    col_blocks = M // col_width

    def add_block(running, block_idx):
        start = (block_idx * col_width).astype(jnp.int32)
        columns = lax.dynamic_slice_in_dim(cov_rows, start, col_width, 1)
        part = lax.dynamic_slice_in_dim(scaled, start, col_width, 1)
        term = lax.dot_general(part, columns, (((1,), (1,)), ((), ())), preferred_element_type=jnp.float32)
        return running + term, None

    initial = jnp.zeros((n_loads, ROWS), jnp.float32)
    result, _ = lax.scan(add_block, initial, jnp.arange(col_blocks, dtype=jnp.int32))
    return result
```

```python
import functools

import jax
import jax.numpy as jnp
from jax import lax
from jax.experimental import pallas as pl
from jax.experimental.pallas import tpu as pltpu
from jax.sharding import PartitionSpec as P

LANES = 128


def remote(src, dst, send_sem, recv_sem, blk, team):
    return pltpu.make_async_remote_copy(
        src_ref=src,
        dst_ref=dst,
        send_sem=send_sem,
        recv_sem=recv_sem,
        device_id={"blk": blk, "team": team},
        device_id_type=pl.DeviceIdType.MESH,
    )


def kernel(
    n_blk,
    n_team,
    load_ref,
    scale_ref,
    cov_ref,
    out_ref,
    cov_buf,
    own,
    held,
    total,
    parts,
    cov_sem,
    hub_sem,
    recv_sem,
    up_sem,
    down_sem,
    side_sem,
    sum_send,
    sum_recv,
):
    n_rows, _, stops, _ = cov_ref.shape
    pieces, n_loads, width = own.shape
    depth = width // LANES
    count = n_team * pieces
    length = n_blk // 2
    blk, team = lax.axis_index("blk"), lax.axis_index("team")
    place = blk // 2
    side = blk + 1 - 2 * (blk % 2)
    relays = (blk % 2) == (team % 2)
    own_stop, own_team = blk // n_team, blk % n_team

    barrier = pltpu.get_barrier_semaphore()

    def greet(b, t):
        pl.semaphore_signal(
            barrier, inc=1, device_id={"blk": b, "team": t}, device_id_type=pl.DeviceIdType.MESH
        )

    for away in range(1, n_team):
        greet(blk, (team + away) % n_team)
    greet(side, team)

    @pl.when(relays & (place > 0))
    def _():
        greet(blk - 2, team)

    @pl.when(relays & (place < length - 1))
    def _():
        greet(blk + 2, team)

    scale = scale_ref[...].astype(jnp.float32).T
    for h in range(pieces):
        cols = []
        for n in range(depth):
            g = h * depth + n
            x = load_ref[:, g * LANES : (g + 1) * LANES].astype(jnp.float32)
            cols.append((x * scale[:, g : g + 1]).astype(jnp.bfloat16))
        own[h] = jnp.concatenate(cols, axis=1) if depth > 1 else cols[0]

    def order(k):
        pair = (team // 2) * 2
        late = jnp.maximum(k - 2 * pieces, 0)
        m_near = pair + (team % 2 + k // pieces) % 2
        m_far = (pair + 2 + late % (n_team - 2)) % n_team
        near = k < 2 * pieces
        m = jnp.where(near, m_near, m_far)
        h = jnp.where(near, k % pieces, late // (n_team - 2))
        return m, m * pieces + h

    ends = jnp.where(place > 0, 1, 0) + jnp.where(place < length - 1, 1, 0)
    pl.semaphore_wait(barrier, n_team + jnp.where(relays, ends, 0))

    def to_hub(h):
        at = team * pieces + h
        return remote(
            own.at[h], held.at[own_stop, at], hub_sem.at[h], recv_sem.at[own_stop, at], blk, own_team
        )

    @pl.when(team != own_team)
    def _():
        for h in range(pieces):
            to_hub(h).start()

    @pl.when(team == own_team)
    def _():
        for h in range(pieces):
            held[own_stop, team * pieces + h] = own[h]

    @pl.loop(0, count)
    def _(k):
        _, at = order(k)

        @pl.loop(0, depth)
        def _(n):
            j = at * depth + n
            pltpu.make_async_copy(cov_ref.at[:, j], cov_buf.at[j], cov_sem.at[at]).start()

    flat = cov_buf.reshape(count * depth, n_rows * stops, LANES)
    total[...] = jnp.zeros_like(total)
    row_stop = lax.broadcasted_iota(jnp.int32, (n_rows * stops, n_loads), 0) % stops

    def where_is(stop):
        block = n_team * stop + team
        home = block // 2
        apart = jnp.where(home > place, home - place, place - home)
        goes_up = relays & (home <= place) & (place < length - 1)
        goes_down = relays & (place <= home) & (place > 0)
        return block, apart, goes_up, goes_down

    def onward(stop, at, sems, b):
        piece = held.at[stop, at]
        return remote(piece, piece, sems.at[stop, at], recv_sem.at[stop, at], b, team)

    @pl.loop(0, count + length - 1)
    def _(step):
        @pl.when(step < count)
        def _():
            _, at = order(step)
            loaded = cov_buf.at[pl.ds(at * depth, depth)]
            pltpu.make_async_copy(loaded, loaded, cov_sem.at[at]).wait()

        @pl.loop(0, stops)
        def _(stop):
            block, apart, goes_up, goes_down = where_is(stop)
            k = step - apart

            @pl.when((k >= 0) & (k < count))
            def _():
                m, at = order(k)

                @pl.when((block != blk) | (m != team))
                def _():
                    onward(stop, at, side_sem, side).wait_recv()

                @pl.when(goes_up)
                def _():
                    onward(stop, at, up_sem, blk + 2).start()

                @pl.when(goes_down)
                def _():
                    onward(stop, at, down_sem, blk - 2).start()

                @pl.when(relays)
                def _():
                    onward(stop, at, side_sem, side).start()

                cov = [flat[at * depth + n] for n in range(depth)]
                cov = jnp.concatenate(cov, axis=1) if depth > 1 else cov[0]
                term = lax.dot_general(
                    cov, held[stop, at], (((1,), (1,)), ((), ())), preferred_element_type=jnp.float32
                )
                total[:, 0:n_loads] += jnp.where(row_stop == stop, term, 0.0)

    part = total[pl.ds(0, n_rows, stride=stops), :]
    for stop in range(1, stops):
        part = part + total[pl.ds(stop, n_rows, stride=stops), :]
    parts[team] = part.T[0:n_loads, :]

    def exchange(away):
        return remote(
            parts.at[team],
            parts.at[team],
            sum_send.at[away],
            sum_recv.at[team],
            blk,
            (team + away) % n_team,
        )

    def arrival(m):
        return remote(parts.at[m], parts.at[m], sum_send.at[0], sum_recv.at[m], blk, m)

    for away in range(1, n_team):
        exchange(away).start()

    @pl.when(team != own_team)
    def _():
        for h in range(pieces):
            to_hub(h).wait_send()

    @pl.loop(0, stops)
    def _(stop):
        _, _, goes_up, goes_down = where_is(stop)

        @pl.loop(0, count)
        def _(at):
            @pl.when(goes_up)
            def _():
                onward(stop, at, up_sem, blk + 2).wait_send()

            @pl.when(goes_down)
            def _():
                onward(stop, at, down_sem, blk - 2).wait_send()

            @pl.when(relays)
            def _():
                onward(stop, at, side_sem, side).wait_send()

    for away in range(1, n_team):
        exchange(away).wait_send()
        arrival((team + away) % n_team).wait_recv()
    result = parts[0]
    for m in range(1, n_team):
        result = result + parts[m]
    out_ref[...] = result


def per_device(n_blk, n_team, loadings, scales, cov):
    n_loads, n_cols = loadings.shape
    n_rows, stops, _, block = cov.shape
    tiles = n_cols // LANES
    pieces = 3 if tiles % 3 == 0 else 1
    width = n_cols // pieces
    count = n_team * pieces
    by_tile = cov[:, :, 0, :].reshape(n_rows, stops, block // LANES, LANES).transpose(0, 2, 1, 3)
    dma = pltpu.SemaphoreType.DMA
    return pl.pallas_call(
        functools.partial(kernel, n_blk, n_team),
        out_shape=jax.ShapeDtypeStruct((n_loads, n_rows), jnp.float32),
        in_specs=[
            pl.BlockSpec(memory_space=pltpu.VMEM),
            pl.BlockSpec(memory_space=pltpu.VMEM),
            pl.BlockSpec(memory_space=pl.ANY),
        ],
        out_specs=pl.BlockSpec(memory_space=pltpu.VMEM),
        scratch_shapes=[
            pltpu.VMEM((block // LANES, n_rows, stops, LANES), jnp.bfloat16),
            pltpu.VMEM((pieces, n_loads, width), jnp.bfloat16),
            pltpu.VMEM((stops, count, n_loads, width), jnp.bfloat16),
            pltpu.VMEM((n_rows * stops, LANES), jnp.float32),
            pltpu.VMEM((n_team, n_loads, n_rows), jnp.float32),
            dma((count,)),
            dma((pieces,)),
            dma((stops, count)),
            dma((stops, count)),
            dma((stops, count)),
            dma((stops, count)),
            dma((n_team,)),
            dma((n_team,)),
        ],
        compiler_params=pltpu.CompilerParams(
            collective_id=0, has_side_effects=True, vmem_limit_bytes=44 << 20
        ),
    )(loadings, scales.T, by_tile)


def solution(mesh):
    placed = (P(None, ("blk", "team")), P(None, ("blk", "team")), P("blk", None, "team", None))
    return jax.shard_map(
        functools.partial(per_device, mesh.shape["blk"], mesh.shape["team"]),
        mesh=mesh,
        in_specs=placed,
        out_specs=P(None, "blk"),
        check_vma=False,
    )
```

```python
import functools

import jax
import jax.numpy as jnp
from jax import lax
from jax.experimental import pallas as pl
from jax.experimental.pallas import tpu as pltpu
from jax.sharding import PartitionSpec as P

LANES = 128
AHEAD = 4


def remote(src, dst, send_sem, recv_sem, blk, team):
    return pltpu.make_async_remote_copy(
        src_ref=src,
        dst_ref=dst,
        send_sem=send_sem,
        recv_sem=recv_sem,
        device_id={"blk": blk, "team": team},
        device_id_type=pl.DeviceIdType.MESH,
    )


def kernel(
    n_blk,
    n_team,
    load_hbm,
    scale_hbm,
    cov_ref,
    out_ref,
    load_ref,
    scale_ref,
    cov_buf,
    own,
    held,
    total,
    parts,
    load_sem,
    cov_sem,
    hub_sem,
    recv_sem,
    up_sem,
    down_sem,
    side_sem,
    sum_send,
    sum_recv,
):
    n_rows, _, stops, _ = cov_ref.shape
    pieces, n_loads, width = own.shape
    depth = width // LANES
    count = n_team * pieces
    length = n_blk // 2
    blk, team = lax.axis_index("blk"), lax.axis_index("team")
    place = blk // 2
    side = blk + 1 - 2 * (blk % 2)
    relays = (blk % 2) == (team % 2)
    own_stop, own_team = blk // n_team, blk % n_team

    barrier = pltpu.get_barrier_semaphore()

    def greet(b, t):
        pl.semaphore_signal(
            barrier, inc=1, device_id={"blk": b, "team": t}, device_id_type=pl.DeviceIdType.MESH
        )

    for away in range(1, n_team):
        greet(blk, (team + away) % n_team)
    greet(side, team)

    @pl.when(relays & (place > 0))
    def _():
        greet(blk - 2, team)

    @pl.when(relays & (place < length - 1))
    def _():
        greet(blk + 2, team)

    loads = pltpu.make_async_copy(load_hbm, load_ref, load_sem.at[0])
    scales = pltpu.make_async_copy(scale_hbm, scale_ref, load_sem.at[1])
    scales.start()
    loads.start()

    def order(k):
        pair = (team // 2) * 2
        late = jnp.maximum(k - 2 * pieces, 0)
        m_near = pair + (team % 2 + k // pieces) % 2
        m_far = (pair + 2 + late % (n_team - 2)) % n_team
        near = k < 2 * pieces
        m = jnp.where(near, m_near, m_far)
        h = jnp.where(near, k % pieces, late // (n_team - 2))
        return m, m * pieces + h

    def fetch(k):
        _, at = order(k)

        @pl.loop(0, depth)
        def _(n):
            j = at * depth + n
            pltpu.make_async_copy(cov_ref.at[:, j], cov_buf.at[j], cov_sem.at[at]).start()

    for k in range(min(AHEAD, count)):
        fetch(k)

    scales.wait()
    loads.wait()
    scale = scale_ref[...].astype(jnp.float32).T
    for h in range(pieces):
        cols = []
        for n in range(depth):
            g = h * depth + n
            x = load_ref[:, g * LANES : (g + 1) * LANES].astype(jnp.float32)
            cols.append((x * scale[:, g : g + 1]).astype(jnp.bfloat16))
        own[h] = jnp.concatenate(cols, axis=1) if depth > 1 else cols[0]

    ends = jnp.where(place > 0, 1, 0) + jnp.where(place < length - 1, 1, 0)
    pl.semaphore_wait(barrier, n_team + jnp.where(relays, ends, 0))

    def to_hub(h):
        at = team * pieces + h
        return remote(
            own.at[h], held.at[own_stop, at], hub_sem.at[h], recv_sem.at[own_stop, at], blk, own_team
        )

    @pl.when(team != own_team)
    def _():
        for h in range(pieces):
            to_hub(h).start()

    @pl.when(team == own_team)
    def _():
        for h in range(pieces):
            held[own_stop, team * pieces + h] = own[h]

    flat = cov_buf.reshape(count * depth, n_rows * stops, LANES)
    total[...] = jnp.zeros_like(total)
    row_stop = lax.broadcasted_iota(jnp.int32, total.shape, 0) % stops
    col_stop = lax.broadcasted_iota(jnp.int32, total.shape, 1) // n_loads
    first, last = team // 2, (n_team // 2) * (stops - 1) + team // 2
    lag = jnp.maximum(
        jnp.where(first > place, first - place, place - first),
        jnp.where(last > place, last - place, place - last),
    )

    def where_is(stop):
        block = n_team * stop + team
        home = block // 2
        apart = jnp.where(home > place, home - place, place - home)
        goes_up = relays & (home <= place) & (place < length - 1)
        goes_down = relays & (place <= home) & (place > 0)
        return block, apart, goes_up, goes_down

    def onward(stop, at, sems, b):
        piece = held.at[stop, at]
        return remote(piece, piece, sems.at[stop, at], recv_sem.at[stop, at], b, team)

    @pl.loop(0, count + length - 1)
    def _(step):
        @pl.loop(0, stops)
        def _(stop):
            block, apart, goes_up, goes_down = where_is(stop)
            k = step - apart

            @pl.when((k >= 0) & (k < count))
            def _():
                m, at = order(k)

                @pl.when((block != blk) | (m != team))
                def _():
                    onward(stop, at, side_sem, side).wait_recv()

                @pl.when(goes_up)
                def _():
                    onward(stop, at, up_sem, blk + 2).start()

                @pl.when(goes_down)
                def _():
                    onward(stop, at, down_sem, blk - 2).start()

                @pl.when(relays)
                def _():
                    onward(stop, at, side_sem, side).start()

        @pl.when(step + AHEAD < count)
        def _():
            fetch(step + AHEAD)

        ready = step - lag

        @pl.when((ready >= 0) & (ready < count))
        def _():
            _, at = order(ready)
            loaded = cov_buf.at[pl.ds(at * depth, depth)]
            pltpu.make_async_copy(loaded, loaded, cov_sem.at[at]).wait()
            cov = [flat[at * depth + n] for n in range(depth)]
            cov = jnp.concatenate(cov, axis=1) if depth > 1 else cov[0]

            @pl.loop(0, stops // 2)
            def _(pair):
                scaled = jnp.concatenate([held[2 * pair, at], held[2 * pair + 1, at]], axis=0)
                term = lax.dot_general(
                    cov, scaled, (((1,), (1,)), ((), ())), preferred_element_type=jnp.float32
                )
                total[...] += jnp.where(row_stop == col_stop + 2 * pair, term, 0.0)

    part = total[pl.ds(0, n_rows, stride=stops), :]
    for stop in range(1, stops):
        part = part + total[pl.ds(stop, n_rows, stride=stops), :]
    part = part.T
    parts[team] = part[0:n_loads, :] + part[n_loads : 2 * n_loads, :]

    def exchange(away):
        return remote(
            parts.at[team],
            parts.at[team],
            sum_send.at[away],
            sum_recv.at[team],
            blk,
            (team + away) % n_team,
        )

    def arrival(m):
        return remote(parts.at[m], parts.at[m], sum_send.at[0], sum_recv.at[m], blk, m)

    for away in range(1, n_team):
        exchange(away).start()

    @pl.when(team != own_team)
    def _():
        for h in range(pieces):
            to_hub(h).wait_send()

    @pl.loop(0, stops)
    def _(stop):
        _, _, goes_up, goes_down = where_is(stop)

        @pl.loop(0, count)
        def _(at):
            @pl.when(goes_up)
            def _():
                onward(stop, at, up_sem, blk + 2).wait_send()

            @pl.when(goes_down)
            def _():
                onward(stop, at, down_sem, blk - 2).wait_send()

            @pl.when(relays)
            def _():
                onward(stop, at, side_sem, side).wait_send()

    for away in range(1, n_team):
        exchange(away).wait_send()
        arrival((team + away) % n_team).wait_recv()
    result = parts[0]
    for m in range(1, n_team):
        result = result + parts[m]
    out_ref[...] = result


def per_device(n_blk, n_team, loadings, scales, cov):
    n_loads, n_cols = loadings.shape
    n_rows, stops, _, block = cov.shape
    tiles = n_cols // LANES
    pieces = max(p for p in (1, 3, 4) if tiles % p == 0)
    width = n_cols // pieces
    count = n_team * pieces
    by_tile = cov[:, :, 0, :].reshape(n_rows, stops, block // LANES, LANES).transpose(0, 2, 1, 3)
    dma = pltpu.SemaphoreType.DMA
    return pl.pallas_call(
        functools.partial(kernel, n_blk, n_team),
        out_shape=jax.ShapeDtypeStruct((n_loads, n_rows), jnp.float32),
        in_specs=[
            pl.BlockSpec(memory_space=pl.ANY),
            pl.BlockSpec(memory_space=pl.ANY),
            pl.BlockSpec(memory_space=pl.ANY),
        ],
        out_specs=pl.BlockSpec(memory_space=pltpu.VMEM),
        scratch_shapes=[
            pltpu.VMEM((n_loads, n_cols), jnp.bfloat16),
            pltpu.VMEM((tiles, n_loads), jnp.bfloat16),
            pltpu.VMEM((block // LANES, n_rows, stops, LANES), jnp.bfloat16),
            pltpu.VMEM((pieces, n_loads, width), jnp.bfloat16),
            pltpu.VMEM((stops, count, n_loads, width), jnp.bfloat16),
            pltpu.VMEM((n_rows * stops, 2 * n_loads), jnp.float32),
            pltpu.VMEM((n_team, n_loads, n_rows), jnp.float32),
            dma((2,)),
            dma((count,)),
            dma((pieces,)),
            dma((stops, count)),
            dma((stops, count)),
            dma((stops, count)),
            dma((stops, count)),
            dma((n_team,)),
            dma((n_team,)),
        ],
        compiler_params=pltpu.CompilerParams(
            collective_id=0, has_side_effects=True, vmem_limit_bytes=56 << 20
        ),
    )(loadings, scales.T, by_tile)


def solution(mesh):
    placed = (P(None, ("blk", "team")), P(None, ("blk", "team")), P("blk", None, "team", None))
    return jax.shard_map(
        functools.partial(per_device, mesh.shape["blk"], mesh.shape["team"]),
        mesh=mesh,
        in_specs=placed,
        out_specs=P(None, "blk"),
        check_vma=False,
    )
```

```python
import functools

import jax
import jax.numpy as jnp
from jax import lax
from jax.experimental import pallas as pl
from jax.experimental.pallas import tpu as pltpu
from jax.sharding import PartitionSpec as P

LANES = 128


def remote(src, dst, send_sem, recv_sem, blk, team):
    return pltpu.make_async_remote_copy(
        src_ref=src,
        dst_ref=dst,
        send_sem=send_sem,
        recv_sem=recv_sem,
        device_id={"blk": blk, "team": team},
        device_id_type=pl.DeviceIdType.MESH,
    )


def kernel(
    n_blk,
    n_team,
    load_hbm,
    scale_hbm,
    cov_ref,
    out_ref,
    load_ref,
    scale_ref,
    cov_buf,
    own,
    held,
    total,
    parts,
    load_sem,
    cov_sem,
    hub_sem,
    recv_sem,
    up_sem,
    down_sem,
    side_sem,
    sum_send,
    sum_recv,
):
    n_rows, _, stops, _ = cov_ref.shape
    pieces, n_loads, width = own.shape
    depth = width // LANES
    count = n_team * pieces
    length = n_blk // 2
    blk, team = lax.axis_index("blk"), lax.axis_index("team")
    place = blk // 2
    side = blk + 1 - 2 * (blk % 2)
    relays = (blk % 2) == (team % 2)
    own_stop, own_team = blk // n_team, blk % n_team

    barrier = pltpu.get_barrier_semaphore()

    def greet(b, t):
        pl.semaphore_signal(
            barrier, inc=1, device_id={"blk": b, "team": t}, device_id_type=pl.DeviceIdType.MESH
        )

    for away in range(1, n_team):
        greet(blk, (team + away) % n_team)
    greet(side, team)

    @pl.when(relays & (place > 0))
    def _():
        greet(blk - 2, team)

    @pl.when(relays & (place < length - 1))
    def _():
        greet(blk + 2, team)

    loads = pltpu.make_async_copy(load_hbm, load_ref, load_sem.at[0])
    scales = pltpu.make_async_copy(scale_hbm, scale_ref, load_sem.at[1])
    scales.start()
    loads.start()

    def order(k):
        pair = (team // 2) * 2
        late = jnp.maximum(k - 2 * pieces, 0)
        m_near = pair + (team % 2 + k // pieces) % 2
        m_far = (pair + 2 + late % (n_team - 2)) % n_team
        near = k < 2 * pieces
        m = jnp.where(near, m_near, m_far)
        h = jnp.where(near, k % pieces, late // (n_team - 2))
        return m, m * pieces + h

    @pl.loop(0, count)
    def _(k):
        _, at = order(k)
        tiles = cov_ref.at[:, pl.ds(at * depth, depth)]
        pltpu.make_async_copy(tiles, cov_buf.at[at], cov_sem.at[at]).start()

    scales.wait()
    loads.wait()
    scale = scale_ref[...].astype(jnp.float32).T
    for h in range(pieces):
        cols = []
        for n in range(depth):
            g = h * depth + n
            x = load_ref[:, g * LANES : (g + 1) * LANES].astype(jnp.float32)
            cols.append((x * scale[:, g : g + 1]).astype(jnp.bfloat16))
        own[h] = jnp.concatenate(cols, axis=1) if depth > 1 else cols[0]

    ends = jnp.where(place > 0, 1, 0) + jnp.where(place < length - 1, 1, 0)
    pl.semaphore_wait(barrier, n_team + jnp.where(relays, ends, 0))

    def to_hub(h):
        at = team * pieces + h
        return remote(
            own.at[h], held.at[own_stop, at], hub_sem.at[h], recv_sem.at[own_stop, at], blk, own_team
        )

    @pl.when(team != own_team)
    def _():
        for h in range(pieces):
            to_hub(h).start()

    @pl.when(team == own_team)
    def _():
        for h in range(pieces):
            held[own_stop, team * pieces + h] = own[h]

    total[...] = jnp.zeros_like(total)
    row_stop = lax.broadcasted_iota(jnp.int32, total.shape, 0) % stops
    col_stop = lax.broadcasted_iota(jnp.int32, total.shape, 1) // n_loads
    first, last = team // 2, (n_team // 2) * (stops - 1) + team // 2
    lag = jnp.maximum(
        jnp.where(first > place, first - place, place - first),
        jnp.where(last > place, last - place, place - last),
    )

    def where_is(stop):
        block = n_team * stop + team
        home = block // 2
        apart = jnp.where(home > place, home - place, place - home)
        goes_up = relays & (home <= place) & (place < length - 1)
        goes_down = relays & (place <= home) & (place > 0)
        return block, apart, goes_up, goes_down

    def onward(stop, at, sems, b):
        piece = held.at[stop, at]
        return remote(piece, piece, sems.at[stop, at], recv_sem.at[stop, at], b, team)

    @pl.loop(0, count + length - 1)
    def _(step):
        @pl.loop(0, stops)
        def _(stop):
            block, apart, goes_up, goes_down = where_is(stop)
            k = step - apart

            @pl.when((k >= 0) & (k < count))
            def _():
                m, at = order(k)

                @pl.when((block != blk) | (m != team))
                def _():
                    onward(stop, at, side_sem, side).wait_recv()

                @pl.when(goes_up)
                def _():
                    onward(stop, at, up_sem, blk + 2).start()

                @pl.when(goes_down)
                def _():
                    onward(stop, at, down_sem, blk - 2).start()

                @pl.when(relays)
                def _():
                    onward(stop, at, side_sem, side).start()

        ready = step - lag

        @pl.when((ready >= 0) & (ready < count))
        def _():
            _, at = order(ready)
            loaded = cov_buf.at[at]
            pltpu.make_async_copy(loaded, loaded, cov_sem.at[at]).wait()
            cov = [cov_buf[at, :, n].reshape(n_rows * stops, LANES) for n in range(depth)]
            cov = jnp.concatenate(cov, axis=1) if depth > 1 else cov[0]

            @pl.loop(0, stops // 2)
            def _(pair):
                scaled = jnp.concatenate([held[2 * pair, at], held[2 * pair + 1, at]], axis=0)
                term = lax.dot_general(
                    cov, scaled, (((1,), (1,)), ((), ())), preferred_element_type=jnp.float32
                )
                total[...] += jnp.where(row_stop == col_stop + 2 * pair, term, 0.0)

    part = total[pl.ds(0, n_rows, stride=stops), :]
    for stop in range(1, stops):
        part = part + total[pl.ds(stop, n_rows, stride=stops), :]
    part = part.T
    parts[team] = part[0:n_loads, :] + part[n_loads : 2 * n_loads, :]

    def exchange(away):
        return remote(
            parts.at[team],
            parts.at[team],
            sum_send.at[away],
            sum_recv.at[team],
            blk,
            (team + away) % n_team,
        )

    def arrival(m):
        return remote(parts.at[m], parts.at[m], sum_send.at[0], sum_recv.at[m], blk, m)

    for away in range(1, n_team):
        exchange(away).start()

    @pl.when(team != own_team)
    def _():
        for h in range(pieces):
            to_hub(h).wait_send()

    @pl.loop(0, stops)
    def _(stop):
        _, _, goes_up, goes_down = where_is(stop)

        @pl.loop(0, count)
        def _(at):
            @pl.when(goes_up)
            def _():
                onward(stop, at, up_sem, blk + 2).wait_send()

            @pl.when(goes_down)
            def _():
                onward(stop, at, down_sem, blk - 2).wait_send()

            @pl.when(relays)
            def _():
                onward(stop, at, side_sem, side).wait_send()

    for away in range(1, n_team):
        exchange(away).wait_send()
        arrival((team + away) % n_team).wait_recv()
    result = parts[0]
    for m in range(1, n_team):
        result = result + parts[m]
    out_ref[...] = result


def per_device(n_blk, n_team, loadings, scales, cov):
    n_loads, n_cols = loadings.shape
    n_rows, stops, _, block = cov.shape
    tiles = n_cols // LANES
    pieces = max(p for p in (1, 3) if tiles % p == 0)
    width = n_cols // pieces
    count = n_team * pieces
    by_tile = cov[:, :, 0, :].reshape(n_rows, stops, block // LANES, LANES).transpose(0, 2, 1, 3)
    dma = pltpu.SemaphoreType.DMA
    return pl.pallas_call(
        functools.partial(kernel, n_blk, n_team),
        out_shape=jax.ShapeDtypeStruct((n_loads, n_rows), jnp.float32),
        in_specs=[
            pl.BlockSpec(memory_space=pl.ANY),
            pl.BlockSpec(memory_space=pl.ANY),
            pl.BlockSpec(memory_space=pl.ANY),
        ],
        out_specs=pl.BlockSpec(memory_space=pltpu.VMEM),
        scratch_shapes=[
            pltpu.VMEM((n_loads, n_cols), jnp.bfloat16),
            pltpu.VMEM((tiles, n_loads), jnp.bfloat16),
            pltpu.VMEM((count, n_rows, width // LANES, stops, LANES), jnp.bfloat16),
            pltpu.VMEM((pieces, n_loads, width), jnp.bfloat16),
            pltpu.VMEM((stops, count, n_loads, width), jnp.bfloat16),
            pltpu.VMEM((n_rows * stops, 2 * n_loads), jnp.float32),
            pltpu.VMEM((n_team, n_loads, n_rows), jnp.float32),
            dma((2,)),
            dma((count,)),
            dma((pieces,)),
            dma((stops, count)),
            dma((stops, count)),
            dma((stops, count)),
            dma((stops, count)),
            dma((n_team,)),
            dma((n_team,)),
        ],
        compiler_params=pltpu.CompilerParams(
            collective_id=0, has_side_effects=True, vmem_limit_bytes=56 << 20
        ),
    )(loadings, scales.T, by_tile)


def solution(mesh):
    placed = (P(None, ("blk", "team")), P(None, ("blk", "team")), P("blk", None, "team", None))
    return jax.shard_map(
        functools.partial(per_device, mesh.shape["blk"], mesh.shape["team"]),
        mesh=mesh,
        in_specs=placed,
        out_specs=P(None, "blk"),
        check_vma=False,
    )
```
